256 devices in a mesh: dp: 16 (over y, x), vocab: 16 (over z, core).
Axes of the slice: x: 4, y: 4, z: 8, core: 2. Of those that a mesh axis runs over, the one named last changes fastest.
Arguments:
- hidden_states: bfloat16 [4096, 1280], P('dp')
- head_weight: bfloat16 [1280, 77824], P('dp', 'vocab')
- teacher_logprobs: bfloat16 [4096, 77824], P('dp', 'vocab'), may hold values from -18 to -2
- teacher_dest: int32 [4096], P('dp'), may hold values from 0 to 4095, as said below
- lengths: int32 [32], P('dp'), may hold values from 21 to 128, as said below
Outputs:
- hidden_grad: float32 [4096, 1280], P('dp', 'vocab')
- token_loss: float32 [4096], P('dp')
The draws below stay inside these ranges and needn't reach their ends.
Inputs may be any that keep to these rules, and one draw needn't show every extreme that they name: teacher_dest is a permutation of the 4096 rollout rows; the 256 teacher rows of each data group go to every data group in equal numbers, 16 to each. `lengths`: sample k covers rollout rows k * 128 to (k + 1) * 128 - 1.
All inputs are finite; a program needn't handle non-finite values.
Results may differ from the reference program's by a relative error of at most 0.004.
Values may be sent and summed in bfloat16 or wider, within the bound.
A program may use at most 128 MiB of HBM per device.

```python
import math
from functools import partial
import jax
import jax.numpy as jnp
from jax import lax

D = 1280
SLOT = 128
SAMP_DEV = 2
VOCAB = 77824
TOK_DEV = 256
TOKENS = 4096
SAMPLES = 32
N_DP = 16


def draw_hidden_states(key, part):
    key = jax.random.fold_in(key, 5)
    first_key = jax.random.fold_in(key, 0)
    states = 3.0 * jax.random.normal(first_key, (TOKENS, D), jnp.float32)
    return states.astype(jnp.bfloat16)


def draw_head_weight(key, part):
    key = jax.random.fold_in(key, 7)
    first_key = jax.random.fold_in(key, 0)
    weights = jax.random.normal(first_key, (D, VOCAB), jnp.float32) / math.sqrt(D)
    return weights.astype(jnp.bfloat16)


def draw_teacher_dest(key, part):
    key = jax.random.fold_in(key, 11)
    send_key, recv_key = jax.random.split(key)
    share_rows = TOK_DEV // N_DP
    send_order = jax.vmap(lambda item: jax.random.permutation(item, TOK_DEV))(jax.random.split(send_key, N_DP))
    recv_order = jax.vmap(lambda item: jax.random.permutation(item, TOK_DEV))(jax.random.split(recv_key, N_DP))
    target_group = send_order // share_rows
    arrival = jnp.arange(N_DP, dtype=jnp.int32)[:, None] * share_rows + send_order % share_rows
    position = recv_order[target_group, arrival]
    return (target_group * TOK_DEV + position).reshape(TOKENS).astype(jnp.int32)


def draw_lengths(key, part):
    key = jax.random.fold_in(key, 23)
    group_ids = jnp.arange(SAMPLES, dtype=jnp.int32) // SAMP_DEV
    highest = SLOT // 3 + (SLOT - SLOT // 3) * group_ids // (N_DP - 1)
    lowest = jnp.maximum(highest // 2, 1)
    drawn = jax.random.randint(key, (SAMPLES,), lowest, highest + 1, dtype=jnp.int32)
    drawn = drawn.at[0].set(max(SLOT // 3 // 2, 1))
    return drawn.at[SAMPLES - 1].set(SLOT)


def level_of(own_key, dims, shards, least, largest):
    loudness, own = 1.0, jax.random.fold_in(own_key, 6)
    for dim, blocks in shards:
        heights = jnp.exp(jax.random.uniform(jax.random.fold_in(own, dim), (blocks,), jnp.float32, least / len(shards), largest / len(shards)))
        loudness = loudness * jnp.repeat(heights, dims[dim] // blocks).reshape([-1 if axis == dim else 1 for axis in range(len(dims))])
    return loudness


def setup_inputs(seed: int = 0) -> dict:
    seeds = jax.random.split(jax.random.key(seed), 6)
    hidden_states = draw_hidden_states(jax.random.fold_in(seeds[5], 71), 0)
    head_weight = draw_head_weight(jax.random.fold_in(seeds[5], 71), 0)
    teacher_logprobs = jnp.clip(-18.0 + 16.0 * jax.random.uniform(seeds[2], (TOKENS, VOCAB), jnp.float32) ** level_of(seeds[2], (TOKENS, VOCAB), ((0, 16), (1, 16)), -0.2, 0.2), -18.0, -2.0).astype(jnp.bfloat16)
    teacher_dest = draw_teacher_dest(jax.random.fold_in(seeds[5], 71), 0)
    lengths = draw_lengths(jax.random.fold_in(seeds[5], 71), 0)
    return {"hidden_states": hidden_states, "head_weight": head_weight, "teacher_logprobs": teacher_logprobs, "teacher_dest": teacher_dest, "lengths": lengths}


def head_block(blocked, head_weight):
    states, aligned, weight = blocked
    logits = jnp.dot(states, head_weight, preferred_element_type=jnp.float32)
    targets = aligned.astype(jnp.float32)
    row_max = jnp.max(logits, axis=1, keepdims=True)
    exponent = jnp.exp(logits - row_max)
    row_total = jnp.sum(exponent, axis=1, keepdims=True)
    moment = jnp.sum(exponent * (logits - targets), axis=1, keepdims=True)
    mean_gap = moment / row_total
    token_loss = weight * (mean_gap - row_max - jnp.log(row_total))[:, 0]
    logit_grad = (weight[:, None] * exponent / row_total * (logits - targets - mean_gap)).astype(jnp.bfloat16)
    hidden_grad = lax.dot_general(logit_grad, head_weight, (((1,), (1,)), ((), ())), preferred_element_type=jnp.float32)
    return hidden_grad, token_loss


def reference(hidden_states, head_weight, teacher_logprobs, teacher_dest, lengths):
    row_ids = jnp.arange(TOKENS, dtype=jnp.int32)
    valid_rows = (row_ids % SLOT < lengths[row_ids // SLOT]).astype(jnp.float32)
    token_weight = valid_rows * (TOKENS / jnp.sum(valid_rows))
    aligned = jnp.zeros_like(teacher_logprobs).at[teacher_dest].set(teacher_logprobs)
    blocked = (hidden_states.reshape(N_DP, TOK_DEV, D), aligned.reshape(N_DP, TOK_DEV, VOCAB), token_weight.reshape(N_DP, TOK_DEV))
    hidden_grad, token_loss = lax.map(partial(head_block, head_weight=head_weight), blocked)
    return hidden_grad.reshape(TOKENS, D), token_loss.reshape(TOKENS)
```

```python
import functools

import jax
import jax.numpy as jnp
from jax import lax
from jax.experimental import pallas as pl
from jax.experimental.pallas import tpu as pltpu
from jax.sharding import PartitionSpec as P

MESH = pl.DeviceIdType.MESH
SLOT = 128
N_DP = 16
N_V = 16
N_Z = 8
TOK = 256
SHARE = 16
FEAT = 1280
FB = 80
VSH = 4864
CB = 1280
Q = 4
ROWS = 32
BIG = 1e30
F32, BF16 = jnp.float32, jnp.bfloat16


def col_start(x):
    return pl.multiple_of((19 * (x // 2) + 9 * (x % 2)) * 128, 128)


def kernel(dest_ref, len_ref, h_hbm, w_hbm, t_hbm, grad_ref, loss_ref,
           tin, hin, wbuf, tord, tbuf, hsend, hbuf, possend, posbuf, sel, sbuf,
           lbuf, gbuf, statcol, ycol, lossbuf, asend, arecv, bsend, brecv,
           part, corebuf, stm, stp, rm, rp, xs, xr, fs, fr,
           lsem, wx_s, wy_s, wf_s, w_r, pos_s, pos_r, hd_s, hd_r, hz_s, hz_r, hc_s, hc_r,
           t_s, t_r, a_s, a_r, b_s, b_r, c_s, c_r, m_s, m_r, p_s, p_r, x_s, x_r, f_s, f_r):
    dp = lax.axis_index("dp")
    v = lax.axis_index("vocab")
    x, y = dp % 4, dp // 4
    z, c = v // 2, v % 2

    def rcopy(src, dst, ss, rs, d, vv):
        return pltpu.make_async_remote_copy(
            src_ref=src, dst_ref=dst, send_sem=ss, recv_sem=rs, device_id=(d, vv), device_id_type=MESH)

    bar = pltpu.get_barrier_semaphore()

    def greet(d, vv):
        pl.semaphore_signal(bar, inc=1, device_id=(d, vv), device_id_type=MESH)

    for i in range(1, N_DP):
        greet((dp + i) % N_DP, v)
    for i in range(4):
        greet(y * 4 + (x + i) % 4, z * 2 + 1 - c)
    for i in range(1, N_Z):
        greet(dp, (z + i) % N_Z * 2 + c)
    pl.semaphore_wait(bar, 15 + 4 + 7)

    def w_x(i):
        xt = (x + i) % 4
        return rcopy(w_hbm.at[:, pl.ds(col_start(xt), CB)], wbuf.at[dp], wx_s.at[i], w_r.at[dp], y * 4 + xt, v)

    def y_to(i):
        return (y + i) % 4 * 4 + x

    def w_own_y(i):
        return rcopy(w_hbm.at[:, pl.ds(col_start(x), CB)], wbuf.at[dp], wy_s.at[0, i // 2], w_r.at[dp], y_to(i), v)

    def w_row_y(j, i):
        b = y * 4 + (x + j) % 4
        return rcopy(wbuf.at[b], wbuf.at[b], wy_s.at[j, i // 2], w_r.at[b], y_to(i), v)

    def w_fwd(j, i):
        b = (y + 4 - i) % 4 * 4 + (x + j) % 4
        return rcopy(wbuf.at[b], wbuf.at[b], wf_s.at[j], w_r.at[b], y_to(i), v)

    def w_arrived(b):
        rcopy(wbuf.at[b], wbuf.at[b], wx_s.at[0], w_r.at[b], dp, v).wait_recv()

    own_w = pltpu.make_async_copy(w_hbm.at[:, pl.ds(col_start(x), CB)], wbuf.at[dp], lsem.at[0])
    get_t = pltpu.make_async_copy(t_hbm, tin, lsem.at[1])
    get_h = pltpu.make_async_copy(h_hbm, hin, lsem.at[2])
    for i in (1, 3, 2):
        w_x(i).start()
    for i in (1, 3):
        w_own_y(i).start()
    own_w.start()
    get_t.start()
    get_h.start()

    drow = jnp.concatenate([dest_ref[0:1, :], dest_ref[1:2, :]], axis=1)
    grp = lax.shift_right_logical(drow, 8)
    pos = (drow & 255).astype(F32)
    member = (grp == lax.broadcasted_iota(jnp.int32, (N_DP, TOK), 0)).astype(BF16)
    upper = (lax.broadcasted_iota(jnp.int32, (TOK, TOK), 0)
             <= lax.broadcasted_iota(jnp.int32, (TOK, TOK), 1)).astype(BF16)
    rank = jnp.dot(member, upper, preferred_element_type=F32)
    slot = lax.broadcasted_iota(jnp.int32, (TOK, N_DP), 0)
    spread = (slot // SHARE == lax.broadcasted_iota(jnp.int32, (TOK, N_DP), 1)).astype(BF16)
    member_s = jnp.dot(spread, member, preferred_element_type=F32)
    rank_s = jnp.dot(spread, rank.astype(BF16), preferred_element_type=F32)
    want = (lax.broadcasted_iota(jnp.int32, (TOK, TOK), 0) % SHARE + 1).astype(F32)
    chosen = jnp.where((member_s > 0.5) & (rank_s == want), 1.0, 0.0)
    sel[...] = chosen.astype(BF16)
    sent = jnp.sum(chosen * pos, axis=1, keepdims=True)
    possend[:, 0:SHARE, :] = jnp.broadcast_to(sent, (TOK, 128)).reshape(N_DP, SHARE, 128)
    len0, len1 = jnp.minimum(len_ref[0], SLOT), jnp.minimum(len_ref[1], SLOT)
    possend[:, SHARE:SHARE + 8, :] = jnp.broadcast_to((len0 + len1).astype(F32), (N_DP, 8, 128))

    def pos_msg(i):
        d = (dp + i) % N_DP
        return rcopy(possend.at[d], posbuf.at[dp], pos_s.at[i], pos_r.at[dp], d, v)

    for i in range(1, N_DP):
        pos_msg(i).start()
    posbuf[pl.ds(dp, 1)] = possend[pl.ds(dp, 1)]

    get_t.wait()

    def order(j, _):
        cols = pl.ds(pl.multiple_of(j * 256, 256), 256)
        res = jnp.dot(sel[...], tin[:, cols], preferred_element_type=F32).astype(BF16)
        tord[:, :, :, cols] = res.reshape(Q, 4, SHARE, 256)
        return 0

    lax.fori_loop(0, VSH // 256, order, 0)

    def t_msg(q, i):
        xt = (x + i) % 4
        return rcopy(tord.at[q, :, :, pl.ds(col_start(xt), CB)], tbuf.at[q, :, x], t_s.at[q, i], t_r.at[q, x], y * 4 + xt, v)

    def t_own(q):
        return pltpu.make_async_copy(tord.at[q, :, :, pl.ds(col_start(x), CB)], tbuf.at[q, :, x], t_s.at[q, 0])

    for i in range(1, N_DP):
        s = (dp + N_DP - i) % N_DP
        rcopy(possend.at[s], posbuf.at[s], pos_s.at[0], pos_r.at[s], dp, v).wait_recv()
    pb = posbuf[:, 0:SHARE, :].reshape(TOK, 128)
    lane = lax.broadcasted_iota(jnp.int32, (TOK, 128), 1).astype(F32)
    sbuf[:, 0:128] = (pb == lane).astype(BF16)
    sbuf[:, 128:256] = (pb == lane + 128.0).astype(BF16)
    get_h.wait()
    for j in range(5):
        hsend[:, j * 256:(j + 1) * 256] = jnp.dot(
            sbuf[...], hin[:, j * 256:(j + 1) * 256], preferred_element_type=F32).astype(BF16)

    def h_msg(i):
        d = (dp + i) % N_DP
        return rcopy(hsend.at[pl.ds(pl.multiple_of(d // 4 * 64, 64), 64)], hbuf.at[v], hd_s.at[i], hd_r.at[0], d, v)

    @pl.when(dp == v)
    def _():
        for i in range(1, N_DP):
            h_msg(i).start()
        hbuf[pl.ds(v, 1)] = hsend[pl.ds(pl.multiple_of(y * 64, 64), 64)].reshape(1, 64, FEAT)

    for i in (1, 3, 2):
        t_msg(0, i).start()
    for q in range(Q):
        t_own(q).start()
    own_w.wait()

    for j in (1, 3, 2):
        w_arrived(y * 4 + (x + j) % 4)
        for i in (1, 3):
            w_row_y(j, i).start()
    for q in range(1, Q):
        for i in (1, 3, 2):
            t_msg(q, i).start()

    def h_z(b, i, k):
        return rcopy(hbuf.at[b], hbuf.at[b], hz_s.at[k], hz_r.at[b], dp, (z + i) % N_Z * 2 + c)

    def h_c(b, k):
        return rcopy(hbuf.at[b], hbuf.at[b], hc_s.at[k], hc_r.at[b], dp, z * 2 + 1 - c)

    def h_arrived(b):
        rcopy(hbuf.at[b], hbuf.at[b], hz_s.at[0], hz_r.at[b], dp, v).wait_recv()

    @pl.when(dp != v)
    def _():
        rcopy(hsend.at[pl.ds(0, 64)], hbuf.at[v], hd_s.at[0], hd_r.at[0], dp, v).wait_recv()

    h_z(v, 1, 0).start()
    h_z(v, N_Z - 1, 1).start()
    h_c(v, 0).start()

    def h_step(s):
        b = (v + N_V - 2 * s) % N_V
        h_arrived(b)
        if s < 4:
            h_z(b, 1, 2 * s).start()
        h_c(b, 2 * s - 1).start()
        if s < 4:
            b = (v + 2 * s) % N_V
            h_arrived(b)
            if s < 3:
                h_z(b, N_Z - 1, 2 * s + 1).start()
            h_c(b, 2 * s).start()

    def w_pass(j, i):
        w_arrived((y + 4 - i) % 4 * 4 + (x + j) % 4)
        w_fwd(j, i).start()

    w_pass(0, 1)
    h_step(1)
    w_pass(1, 1)
    w_pass(3, 3)
    h_step(2)
    w_pass(2, 3)
    h_step(3)
    h_step(4)
    for j in (2, 3):
        w_arrived((y + 3) % 4 * 4 + (x + j) % 4)
    for j in (0, 1):
        w_arrived((y + 1) % 4 * 4 + (x + j) % 4)
    for k in range(N_Z):
        b = k * 2 + 1 - c
        rcopy(hbuf.at[b], hbuf.at[b], hc_s.at[0], hc_r.at[b], dp, v).wait_recv()
    for j in range(4):
        w_arrived((y + 2) % 4 * 4 + (x + j) % 4)

    odd = x % 2
    lane_r = lax.broadcasted_iota(jnp.int32, (ROWS, 128), 1)
    me8 = x * 2 + c

    def a_msg(q, i):
        k = (me8 + i) % 8
        return rcopy(asend.at[q], arecv.at[q, me8], a_s.at[q, i], a_r.at[q, me8], y * 4 + k // 2, z * 2 + k % 2)

    def b_msg(q, i):
        return rcopy(bsend.at[q], brecv.at[q, z], b_s.at[q, i], b_r.at[q, z], dp, (z + i) % N_Z * 2 + c)

    def c_msg(q):
        return rcopy(part.at[q, :, 1 - c], corebuf.at[q], c_s.at[q], c_r.at[q], dp, z * 2 + 1 - c)

    def m_msg(q, s):
        return rcopy(stm.at[q, s], rm.at[q, s], m_s.at[q, s], m_r.at[q, s], dp, (z + N_Z - 1) % N_Z * 2 + c)

    def p_msg(q, s):
        return rcopy(stp.at[q, s], rp.at[q, s], p_s.at[q, s], p_r.at[q, s], dp, (z + 1) % N_Z * 2 + c)

    def x_msg(q, i):
        xt = (x + i) % 4
        return rcopy(xs.at[q, xt], xr.at[q, x], x_s.at[q, i], x_r.at[q, x], y * 4 + xt, v)

    def f_msg(q):
        return rcopy(fs.at[q], fr.at[y], f_s.at[q], f_r.at[y], q * 4 + x, v)

    def combine(got):
        halves = []
        for r in (0, 4):
            mxs = got[:, r:r + 1, :]
            mx = jnp.max(mxs, axis=0)
            scale = jnp.exp(mxs - mx[None])
            halves.append((mx, jnp.sum(scale * got[:, r + 1:r + 2, :], axis=0),
                           jnp.sum(scale * got[:, r + 2:r + 3, :], axis=0)))
        return halves

    def stage0(q):
        t_own(q).wait()
        for i in (1, 3, 2):
            s = (x + 4 - i) % 4
            rcopy(tord.at[q, :, :, pl.ds(0, CB)], tbuf.at[q, :, s], t_s.at[q, 0], t_r.at[q, s], dp, v).wait_recv()
        hq = hbuf[pl.ds(q * 4, 4)].reshape(TOK, FEAT)
        for j in range(5):
            wj = wbuf[:, :, j * 256:(j + 1) * 256].reshape(FEAT, 256)
            out = jnp.dot(hq, wj, preferred_element_type=F32)
            if j == 0:
                hidden = (lax.broadcasted_iota(jnp.int32, (TOK, 256), 1) < 128) & (odd == 1)
                out = jnp.where(hidden, -BIG, out)
            lbuf[q, :, j * 256:(j + 1) * 256] = out

        def rows(r, _):
            at = pl.ds(pl.multiple_of(r * ROWS, ROWS), ROWS)
            logits = lbuf[q, at, :]
            targets = tbuf[q, r // 2, pl.ds(r % 2 * 2, 2)].reshape(ROWS, CB).astype(F32)
            mx = jnp.max(logits, axis=1, keepdims=True)
            e = jnp.exp(logits - mx)
            tot = jnp.sum(e, axis=1, keepdims=True)
            mom = jnp.sum(e * (logits - targets), axis=1, keepdims=True)
            base = r // 4 * 4
            statcol[at, :] = jnp.where(lane_r == base, mx, jnp.where(
                lane_r == base + 1, tot, jnp.where(lane_r == base + 2, mom, 0.0)))
            return 0

        lax.fori_loop(0, TOK // ROWS, rows, 0)
        packed = (statcol[0:128, :] + statcol[128:256, :]).T[0:8, :]
        asend[q] = packed
        for i in range(1, 8):
            a_msg(q, i).start()
        arecv[q, pl.ds(me8, 1)] = packed[None]

    def stage1(q):
        for i in range(1, 8):
            s = (me8 + i) % 8
            rcopy(asend.at[q], arecv.at[q, s], a_s.at[q, 0], a_r.at[q, s], dp, v).wait_recv()
        (m0, t0, o0), (m1, t1, o1) = combine(arecv[q])
        pad = jnp.zeros((1, 128), F32)
        packed = jnp.concatenate([m0, t0, o0, pad, m1, t1, o1, pad], axis=0)
        bsend[q] = packed
        for i in range(1, N_Z):
            b_msg(q, i).start()
        brecv[q, pl.ds(z, 1)] = packed[None]

    def stage2(q):
        for i in range(1, N_Z):
            s = (z + i) % N_Z
            rcopy(bsend.at[q], brecv.at[q, s], b_s.at[q, 0], b_r.at[q, s], dp, v).wait_recv()
        rows8 = []
        for mx, tot, mom in combine(brecv[q]):
            gap = mom / tot
            rows8 += [mx, 1.0 / tot, gap, gap - mx - jnp.log(tot)]
        cols = jnp.concatenate(rows8 + [jnp.zeros((120, 128), F32)], axis=0).T
        ycol[...] = cols
        lane_f = lax.broadcasted_iota(jnp.int32, (128, 128), 1)
        for half in range(2):
            lossbuf[q, half * 128:(half + 1) * 128, :] = jnp.where(
                lane_f == FB, cols[:, 4 * half + 3:4 * half + 4], 0.0)

            def rows(r, _, half=half):
                yat = pl.ds(pl.multiple_of(r * ROWS, ROWS), ROWS)
                at = pl.ds(pl.multiple_of(half * 128 + r * ROWS, ROWS), ROWS)
                rr = half * 4 + r
                yc = ycol[yat, :]
                mx, inv, gap = (yc[:, 4 * half + k:4 * half + k + 1] for k in range(3))
                logits = lbuf[q, at, :]
                targets = tbuf[q, rr // 2, pl.ds(rr % 2 * 2, 2)].reshape(ROWS, CB).astype(F32)
                gbuf[at, :] = (jnp.exp(logits - mx) * inv * (logits - targets - gap)).astype(BF16)
                return 0

            lax.fori_loop(0, 4, rows, 0)

        def grads(j, _):
            wj = wbuf[pl.ds(j * 4, 4)].reshape(4 * FB, CB)
            out = lax.dot_general(wj, gbuf[...], (((1,), (1,)), ((), ())), preferred_element_type=F32)
            part[q, pl.ds(j * 2, 2)] = out.reshape(2, 2, FB, TOK)
            return 0

        lax.fori_loop(0, 4, grads, 0)
        c_msg(q).start()

    def own(q, dz):
        d = (z + dz) % N_Z
        return part[q, d, c] + corebuf[q, d]

    def stage3(q):
        c_msg(q).wait_recv()
        stm[q, 0] = own(q, 4).astype(BF16)
        m_msg(q, 0).start()
        stp[q, 0] = own(q, 3).astype(BF16)
        p_msg(q, 0).start()

    def ring(q, s):
        m_msg(q, s - 1).wait_recv()
        stm[q, s] = (rm[q, s - 1].astype(F32) + own(q, 4 + s)).astype(BF16)
        m_msg(q, s).start()
        if s < 3:
            p_msg(q, s - 1).wait_recv()
            stp[q, s] = (rp[q, s - 1].astype(F32) + own(q, 3 - s)).astype(BF16)
            p_msg(q, s).start()

    def stage7(q):
        p_msg(q, 2).wait_recv()
        m_msg(q, 3).wait_recv()
        total = own(q, 0) + rp[q, 2].astype(F32) + rm[q, 3].astype(F32)
        padded = jnp.concatenate([total, jnp.zeros((128 - FB, TOK), F32)], axis=0)
        xs[q] = padded.T.reshape(4, 64, 128)
        for i in (1, 3, 2):
            x_msg(q, i).start()

    def stage8(q):
        total = xs[q, x] + lossbuf[q, pl.ds(pl.multiple_of(x * 64, 64), 64), :]
        for i in (1, 3, 2):
            s = (x + i) % 4
            rcopy(xs.at[q, 0], xr.at[q, s], x_s.at[q, 0], x_r.at[q, s], dp, v).wait_recv()
            total += xr[q, s]
        fs[q] = total

        @pl.when(y == q)
        def _():
            fr[pl.ds(y, 1)] = total[None]

        @pl.when(y != q)
        def _():
            f_msg(q).start()

    stages = [stage0, stage1, stage2, stage3, lambda q: ring(q, 1), lambda q: ring(q, 2), lambda q: ring(q, 3),
              stage7, stage8]

    def tick(tau, _):
        for s in reversed(range(len(stages))):
            q = tau - s

            @pl.when((q >= 0) & (q < Q))
            def _(s=s, q=q):
                stages[s](q)
        return 0

    lax.fori_loop(0, Q + len(stages) - 1, tick, 0)

    for i in range(1, 4):
        s = (y + i) % 4
        rcopy(fs.at[0], fr.at[s], f_s.at[0], f_r.at[s], dp, v).wait_recv()
    rows = fr[...].reshape(TOK, 128)
    hi = rows.astype(BF16)
    rest = rows - hi.astype(F32)
    mid = rest.astype(BF16)
    low = (rest - mid.astype(F32)).astype(BF16)
    placed = jnp.zeros((TOK, 128), F32)
    for piece in (low, mid, hi):
        placed += lax.dot_general(sbuf[...], piece, (((0,), (0,)), ((), ())), preferred_element_type=F32)
    count = jnp.sum(posbuf[:, SHARE:SHARE + 8, :], axis=0)[0:1, :]
    scale = float(TOK * N_DP) / count
    row = lax.broadcasted_iota(jnp.int32, (TOK, 128), 0)
    limit = jnp.where(row < SLOT, len0, len1)
    placed = jnp.where(row % SLOT < limit, placed * scale, 0.0)
    grad_ref[...] = placed[:, 0:FB]
    loss_ref[...] = placed.T[FB:FB + 1, :]

    for i in range(1, 4):
        w_x(i).wait_send()
    for i in (1, 3):
        w_own_y(i).wait_send()
        for j in range(1, 4):
            w_row_y(j, i).wait_send()
    for j, i in ((0, 1), (1, 1), (3, 3), (2, 3)):
        w_fwd(j, i).wait_send()
    for i in range(1, N_DP):
        pos_msg(i).wait_send()

    @pl.when(dp == v)
    def _():
        for i in range(1, N_DP):
            h_msg(i).wait_send()

    for k in range(7):
        h_z(v, 1, k).wait_send()
    for k in range(8):
        h_c(v, k).wait_send()

    def drain(q, _):
        for i in range(1, 4):
            t_msg(q, i).wait_send()
            x_msg(q, i).wait_send()
        for i in range(1, 8):
            a_msg(q, i).wait_send()
            b_msg(q, i).wait_send()
        c_msg(q).wait_send()
        for s in range(4):
            m_msg(q, s).wait_send()
        for s in range(3):
            p_msg(q, s).wait_send()

        @pl.when(y != q)
        def _():
            f_msg(q).wait_send()
        return 0

    lax.fori_loop(0, Q, drain, 0)


def per_device(hidden_states, head_weight, teacher_logprobs, teacher_dest, lengths):
    vm = pltpu.VMEM
    dma = pltpu.SemaphoreType.DMA
    grad, loss = pl.pallas_call(
        kernel,
        out_shape=(jax.ShapeDtypeStruct((TOK, FB), F32), jax.ShapeDtypeStruct((1, TOK), F32)),
        in_specs=[pl.BlockSpec(memory_space=pltpu.VMEM), pl.BlockSpec(memory_space=pltpu.SMEM)]
        + [pl.BlockSpec(memory_space=pl.ANY)] * 3,
        out_specs=(pl.BlockSpec(memory_space=pltpu.VMEM), pl.BlockSpec(memory_space=pltpu.VMEM)),
        scratch_shapes=[
            vm((TOK, VSH), BF16),
            vm((TOK, FEAT), BF16),
            vm((N_DP, FB, CB), BF16),
            vm((Q, 4, SHARE, VSH), BF16),
            vm((Q, 4, 4, SHARE, CB), BF16),
            vm((TOK, FEAT), BF16),
            vm((N_DP, 64, FEAT), BF16),
            vm((N_DP, SHARE + 8, 128), F32),
            vm((N_DP, SHARE + 8, 128), F32),
            vm((TOK, TOK), BF16),
            vm((TOK, TOK), BF16),
            vm((Q, TOK, CB), F32),
            vm((TOK, CB), BF16),
            vm((TOK, 128), F32),
            vm((128, 128), F32),
            vm((Q, TOK, 128), F32),
            vm((Q, 8, 128), F32),
            vm((Q, 8, 8, 128), F32),
            vm((Q, 8, 128), F32),
            vm((Q, N_Z, 8, 128), F32),
            vm((Q, N_Z, 2, FB, TOK), F32),
            vm((Q, N_Z, FB, TOK), F32),
            vm((Q, 4, FB, TOK), BF16),
            vm((Q, 3, FB, TOK), BF16),
            vm((Q, 4, FB, TOK), BF16),
            vm((Q, 3, FB, TOK), BF16),
            vm((Q, 4, 64, 128), F32),
            vm((Q, 4, 64, 128), F32),
            vm((Q, 64, 128), F32),
            vm((4, 64, 128), F32),
            dma((3,)),
            dma((4,)), dma((4, 2)), dma((4,)), dma((N_DP,)),
            dma((N_DP,)), dma((N_DP,)),
            dma((N_DP,)), dma((1,)),
            dma((8,)), dma((N_V,)),
            dma((8,)), dma((N_V,)),
            dma((Q, 4)), dma((Q, 4)),
            dma((Q, 8)), dma((Q, 8)),
            dma((Q, N_Z)), dma((Q, N_Z)),
            dma((Q,)), dma((Q,)),
            dma((Q, 4)), dma((Q, 4)),
            dma((Q, 3)), dma((Q, 3)),
            dma((Q, 4)), dma((Q, 4)),
            dma((Q,)), dma((4,)),
        ],
        compiler_params=pltpu.CompilerParams(
            collective_id=0, has_side_effects=True, vmem_limit_bytes=58 * 2**20),
        name="distill",
    )(teacher_dest.reshape(2, 128), lengths, hidden_states, head_weight, teacher_logprobs)
    return grad, loss.reshape(TOK)


def solution(mesh):
    placed = (P("dp", None), P("dp", "vocab"), P("dp", "vocab"), P("dp"), P("dp"))
    return jax.shard_map(
        per_device,
        mesh=mesh,
        in_specs=placed,
        out_specs=(P("dp", "vocab"), P("dp")),
        check_vma=False,
    )
```

```python
import functools

import jax
import jax.numpy as jnp
from jax import lax
from jax.experimental import pallas as pl
from jax.experimental.pallas import tpu as pltpu
from jax.sharding import PartitionSpec as P

MESH = pl.DeviceIdType.MESH
SLOT = 128
N_DP = 16
N_V = 16
N_Z = 8
TOK = 256
SHARE = 16
FEAT = 1280
FB = 80
VSH = 4864
CB = 1280
CC, NC = 256, 5
Q = 4
ROWS = 32
BIG = 1e30
F32, BF16 = jnp.float32, jnp.bfloat16


def col_start(x):
    return pl.multiple_of((19 * (x // 2) + 9 * (x % 2)) * 128, 128)


def kernel(dest_ref, len_ref, h_hbm, w_hbm, t_hbm, out_ref, place_ref,
           tin, hin, wbuf, tord, tbuf, hsend, hbuf, possend, posbuf, sel, vbuf,
           lbuf, gbuf, statcol, ycol, lossbuf, asend, arecv, bsend, brecv,
           part, corebuf, xs, xr, zs, zr, tr, fs, fr,
           lsem, w_s, wx_r, wf_r, w_r, pos_s, pos_r, hd_s, hd_r, h_s, hz_r, hc_r,
           t_s, t_r, a_s, a_r, b_s, b_r, c_s, c_r, x_s, x_r, z_s, z_r, f_s, f_r):
    dp = lax.axis_index("dp")
    v = lax.axis_index("vocab")
    x, y = dp % 4, dp // 4
    z, c = v // 2, v % 2

    def rcopy(src, dst, ss, rs, d, vv):
        return pltpu.make_async_remote_copy(
            src_ref=src, dst_ref=dst, send_sem=ss, recv_sem=rs, device_id=(d, vv), device_id_type=MESH)

    bar = pltpu.get_barrier_semaphore()

    def greet(d, vv):
        pl.semaphore_signal(bar, inc=1, device_id=(d, vv), device_id_type=MESH)

    for i in range(1, N_DP):
        greet((dp + i) % N_DP, v)
    for i in range(4):
        greet(y * 4 + (x + i) % 4, z * 2 + 1 - c)
    for i in range(1, N_Z):
        greet(dp, (z + i) % N_Z * 2 + c)

    own_w = pltpu.make_async_copy(w_hbm.at[:, pl.ds(col_start(x), CB)], wbuf.at[dp], lsem.at[0])
    get_t = pltpu.make_async_copy(t_hbm, tin, lsem.at[1])
    get_h = pltpu.make_async_copy(h_hbm, hin, lsem.at[2])
    get_t.start()
    own_w.start()
    get_h.start()

    drow = jnp.concatenate([dest_ref[0:1, :], dest_ref[1:2, :]], axis=1)
    grp = lax.shift_right_logical(drow, 8)
    pos = (drow & 255).astype(F32)
    member = (grp == lax.broadcasted_iota(jnp.int32, (N_DP, TOK), 0)).astype(BF16)
    upper = (lax.broadcasted_iota(jnp.int32, (TOK, TOK), 0)
             <= lax.broadcasted_iota(jnp.int32, (TOK, TOK), 1)).astype(BF16)
    rank = jnp.dot(member, upper, preferred_element_type=F32)
    slot = lax.broadcasted_iota(jnp.int32, (TOK, N_DP), 0)
    spread = (slot // SHARE == lax.broadcasted_iota(jnp.int32, (TOK, N_DP), 1)).astype(BF16)
    member_s = jnp.dot(spread, member, preferred_element_type=F32)
    rank_s = jnp.dot(spread, rank.astype(BF16), preferred_element_type=F32)
    want = (lax.broadcasted_iota(jnp.int32, (TOK, TOK), 0) % SHARE + 1).astype(F32)
    chosen = jnp.where((member_s > 0.5) & (rank_s == want), 1.0, 0.0)
    sel[...] = chosen.astype(BF16)
    sent = jnp.sum(chosen * pos, axis=1, keepdims=True)
    lane0 = dp % 8 * SHARE
    lane_s = lax.broadcasted_iota(jnp.int32, (TOK, 128), 1)
    slot_s = lax.broadcasted_iota(jnp.int32, (TOK, 128), 0)
    laid = jnp.where(lane_s == lane0 + slot_s % SHARE, sent, 0.0).astype(BF16)
    by_group = (lax.broadcasted_iota(jnp.int32, (N_DP, TOK), 1) // SHARE
                == lax.broadcasted_iota(jnp.int32, (N_DP, TOK), 0)).astype(BF16)
    rows_out = jnp.dot(by_group, laid, preferred_element_type=F32)
    sub = lax.broadcasted_iota(jnp.int32, (N_DP, 8, 128), 1)
    lane3 = lax.broadcasted_iota(jnp.int32, (N_DP, 8, 128), 2)
    mine = (lane3 >= lane0) & (lane3 < lane0 + SHARE)
    len0 = jnp.minimum(len_ref[0], SLOT).astype(F32)
    len1 = jnp.minimum(len_ref[1], SLOT).astype(F32)
    possend[...] = jnp.where(sub == 0, rows_out.reshape(N_DP, 1, 128), jnp.where(
        mine, jnp.where(sub == 1, len0, jnp.where(sub == 2, len1, 0.0)), 0.0))

    def pos_msg(i):
        d = (dp + i) % N_DP
        return rcopy(possend.at[d], posbuf.at[dp], pos_s.at[0], pos_r.at[0], d, v)

    def cut(j):
        return pl.ds(j * CC, CC)

    def w_cols(xt, j):
        return pl.ds(pl.multiple_of(col_start(xt) + j * CC, 128), CC)

    def w_x(j, i):
        xt = (x + i) % 4
        return rcopy(w_hbm.at[:, w_cols(xt, j)], wbuf.at[dp, :, cut(j)], w_s.at[0], wx_r.at[j], y * 4 + xt, v)

    def y_to(i):
        return (y + i) % 4 * 4 + x

    def w_sem(j, k, i):
        if i == 1 and k in (0, 1):
            return wf_r.at[j, 0]
        if i == 3 and k in (2, 3):
            return wf_r.at[j, 1]
        return w_r.at[j]

    def w_own_y(j, i):
        return rcopy(w_hbm.at[:, w_cols(x, j)], wbuf.at[dp, :, cut(j)], w_s.at[0], w_sem(j, 0, i), y_to(i), v)

    def w_row_y(j, k, i):
        b = y * 4 + (x + k) % 4
        return rcopy(wbuf.at[b, :, cut(j)], wbuf.at[b, :, cut(j)], w_s.at[0], w_sem(j, k, i), y_to(i), v)

    def w_fwd(j, k, i):
        b = (y + 4 - i) % 4 * 4 + (x + k) % 4
        return rcopy(wbuf.at[b, :, cut(j)], wbuf.at[b, :, cut(j)], w_s.at[0], w_r.at[j], y_to(i), v)

    def w_arrived(j, n, sem):
        rcopy(wbuf.at[0:n, :, cut(j)], wbuf.at[0:n, :, cut(j)], w_s.at[0], sem, dp, v).wait_recv()

    pl.semaphore_wait(bar, 15 + 4 + 7)
    for i in range(1, N_DP):
        pos_msg(i).start()
    for j in range(NC):
        for i in (1, 3, 2):
            w_x(j, i).start()
        for i in (1, 3):
            w_own_y(j, i).start()
    posbuf[pl.ds(dp, 1)] = possend[pl.ds(dp, 1)]

    get_t.wait()

    def order(j, _):
        cols = pl.ds(pl.multiple_of(j * 256, 256), 256)
        res = jnp.dot(sel[...], tin[:, cols], preferred_element_type=F32).astype(BF16)
        tord[:, :, :, cols] = res.reshape(Q, 4, SHARE, 256)
        return 0

    lax.fori_loop(0, VSH // 256, order, 0)

    def t_msg(q, i):
        xt = (x + i) % 4
        return rcopy(tord.at[q, :, :, pl.ds(col_start(xt), CB)], tbuf.at[q, :, x], t_s.at[0], t_r.at[q], y * 4 + xt, v)

    t_own = pltpu.make_async_copy(tord.at[:, :, :, pl.ds(col_start(x), CB)], tbuf.at[:, :, x], lsem.at[1])
    t_own.start()

    def unit(vv):
        return vv % 4 * 4 + vv // 4

    rcopy(possend.at[0:15], posbuf.at[0:15], pos_s.at[0], pos_r.at[0], dp, v).wait_recv()
    low_t = jnp.sum(posbuf[0:8], axis=0)
    high_t = jnp.sum(posbuf[8:16], axis=0)
    seen = jnp.concatenate([low_t, high_t], axis=1)
    place = (lax.broadcasted_iota(jnp.int32, (TOK, TOK), 0).astype(F32) == seen[0:1, :]).astype(BF16)
    place_ref[...] = place
    get_h.wait()
    for j in range(5):
        hsend[:, j * 256:(j + 1) * 256] = lax.dot_general(
            place, hin[:, j * 256:(j + 1) * 256], (((0,), (0,)), ((), ())), preferred_element_type=F32).astype(BF16)

    def h_msg(i):
        d = (dp + i) % N_DP
        at = pl.ds(pl.multiple_of((d // 4 * 4 + v // 4) * SHARE, SHARE), SHARE)
        return rcopy(hsend.at[at], hbuf.at[y, unit(v)], hd_s.at[0], hd_r.at[y], d, v)

    @pl.when(x == v % 4)
    def _():
        for i in range(1, N_DP):
            h_msg(i).start()
        hbuf[pl.ds(y, 1), pl.ds(unit(v), 1)] = hsend[
            pl.ds(pl.multiple_of((y * 4 + v // 4) * SHARE, SHARE), SHARE)].reshape(1, 1, SHARE, FEAT)

    sent_row = jnp.broadcast_to(sent, (TOK, 128)).T[0:1, :]
    sent_in = jnp.where(sent_row >= SLOT, sent_row - SLOT, sent_row)
    valid = (sent_in < jnp.where(sent_row >= SLOT, seen[2:3, :], seen[1:2, :])).astype(F32)
    eighth = (lax.broadcasted_iota(jnp.int32, (8, TOK), 1) // 32
              == lax.broadcasted_iota(jnp.int32, (8, TOK), 0)).astype(F32)
    to_lane = (lane_s == slot_s // SHARE % 2 * 64 + x * SHARE + slot_s % SHARE).astype(BF16)
    valid8 = jnp.dot((eighth * valid).astype(BF16), to_lane, preferred_element_type=F32)
    valid8 = jnp.where(c == 0, valid8, 0.0)
    sub8 = lax.broadcasted_iota(jnp.int32, (8, 128), 0)
    for q in range(Q):
        vbuf[q] = jnp.where(sub8 == 3, valid8[2 * q:2 * q + 1, :], jnp.where(
            sub8 == 7, valid8[2 * q + 1:2 * q + 2, :], 0.0))
    count = jnp.sum(seen[1:3, :], keepdims=True) * (1.0 / SHARE)
    scale = float(TOK * N_DP) / count

    own_w.wait()

    def w_pass_x(j):
        w_arrived(j, 3, wx_r.at[j])
        for k in (1, 3, 2):
            for i in (1, 3):
                w_row_y(j, k, i).start()

    def w_pass_y(j):
        for way, (ks, i) in enumerate((((0, 1), 1), ((3, 2), 3))):
            w_arrived(j, 2, wf_r.at[j, way])
            for k in ks:
                w_fwd(j, k, i).start()

    def h_z(h, b, i, s):
        u = unit(b)
        at = hbuf.at[2 * h:2 * h + 2, u]
        return rcopy(at, at, h_s.at[0], hz_r.at[h, i // 4, s], dp, (z + i) % N_Z * 2 + c)

    def h_c(h, b):
        at = hbuf.at[2 * h:2 * h + 2, unit(b)]
        return rcopy(at, at, h_s.at[0], hc_r.at[0], dp, z * 2 + 1 - c)

    def h_first(h):
        for q in (2 * h, 2 * h + 1):
            @pl.when((x != v % 4) | (y != q))
            def _(q=q):
                rcopy(hsend.at[pl.ds(0, SHARE)], hbuf.at[q, unit(v)], hd_s.at[0], hd_r.at[q], dp, v).wait_recv()
        h_z(h, v, 1, 0).start()
        h_z(h, v, N_Z - 1, 0).start()
        h_c(h, v).start()

    def h_step(h, s):
        for way, i in ((0, 1), (1, N_Z - 1)):
            if s == 4 and way != h:
                continue
            b = (v + N_V + (2 * s if way else -2 * s)) % N_V
            h_z(h, b, i, s - 1).wait_recv()
            if s < 3 or (s == 3 and way == h):
                h_z(h, b, i, s).start()
            h_c(h, b).start()

    def t_send(q):
        for i in (1, 3, 2):
            t_msg(q, i).start()

    for j in range(NC):
        w_pass_x(j)
        if j == 2:
            t_send(0)
    for q in range(1, Q):
        t_send(q)
    h_first(0)
    h_first(1)
    w_pass_y(0)
    w_pass_y(1)
    h_step(0, 1)
    h_step(1, 1)
    w_pass_y(2)
    h_step(0, 2)
    h_step(1, 2)
    w_pass_y(3)
    w_pass_y(4)
    h_step(0, 3)
    h_step(1, 3)
    h_step(0, 4)
    h_step(1, 4)
    rcopy(hbuf.at[:, 0:8], hbuf.at[:, 0:8], h_s.at[0], hc_r.at[0], dp, v).wait_recv()

    odd = x % 2
    for j in range(NC):
        w_arrived(j, 8, w_r.at[j])

        def chunk(q, _, j=j):
            wj = wbuf[:, :, j * CC:(j + 1) * CC].reshape(FEAT, CC)
            out = jnp.dot(hbuf[pl.ds(q * 2, 2)].reshape(2 * TOK, FEAT), wj, preferred_element_type=F32)
            if j == 0:
                hidden = (lax.broadcasted_iota(jnp.int32, (2 * TOK, CC), 1) < 128) & (odd == 1)
                out = jnp.where(hidden, -BIG, out)
            lbuf[pl.ds(q * 2, 2), :, j * CC:(j + 1) * CC] = out.reshape(2, TOK, CC)
            return 0

        lax.fori_loop(0, 2, chunk, 0)

    lane_r = lax.broadcasted_iota(jnp.int32, (ROWS, 128), 1)
    me8 = x * 2 + c

    t_own.wait()

    def a_msg(q, i):
        k = (me8 + i) % 8
        return rcopy(asend.at[q], arecv.at[q, me8], a_s.at[0], a_r.at[q], y * 4 + k // 2, z * 2 + k % 2)

    def b_msg(q, i):
        return rcopy(bsend.at[q], brecv.at[q, z], b_s.at[0], b_r.at[q], dp, (z + i) % N_Z * 2 + c)

    def c_msg(q):
        return rcopy(part.at[q, :, 1 - c], corebuf.at[q], c_s.at[0], c_r.at[q], dp, z * 2 + 1 - c)

    def x_msg(q, i):
        xt = (x + i) % 4
        return rcopy(xs.at[q, xt], xr.at[q, x], x_s.at[0], x_r.at[q], y * 4 + xt, v)

    def z_msg(q, i):
        zt = (z + i) % N_Z
        return rcopy(zs.at[q, zt // 2], zr.at[q, z], z_s.at[0], z_r.at[q], dp, zt * 2 + c)

    def f_msg(q):
        return rcopy(fs.at[q], fr.at[y], f_s.at[0], f_r.at[0], q * 4 + x, v)

    def combine(got):
        halves = []
        for r in (0, 4):
            mxs = got[:, r:r + 1, :]
            mx = jnp.max(mxs, axis=0)
            ratio = jnp.exp(mxs - mx[None])
            halves.append((mx, jnp.sum(ratio * got[:, r + 1:r + 2, :], axis=0),
                           jnp.sum(ratio * got[:, r + 2:r + 3, :], axis=0)))
        return halves

    def stage0(q):
        rcopy(tbuf.at[q, :, 0:3], tbuf.at[q, :, 0:3], t_s.at[0], t_r.at[q], dp, v).wait_recv()

        def rows(r, _):
            at = pl.ds(pl.multiple_of(r * ROWS, ROWS), ROWS)
            logits = lbuf[q, at, :]
            targets = tbuf[q, r // 2, pl.ds(r % 2 * 2, 2)].reshape(ROWS, CB).astype(F32)
            mx = jnp.max(logits, axis=1, keepdims=True)
            e = jnp.exp(logits - mx)
            tot = jnp.sum(e, axis=1, keepdims=True)
            mom = jnp.sum(e * (logits - targets), axis=1, keepdims=True)
            base = r // 4 * 4
            statcol[at, :] = jnp.where(lane_r == base, mx, jnp.where(
                lane_r == base + 1, tot, jnp.where(lane_r == base + 2, mom, 0.0)))
            return 0

        lax.fori_loop(0, TOK // ROWS, rows, 0, unroll=4)
        packed = (statcol[0:128, :] + statcol[128:256, :]).T[0:8, :] + vbuf[q]
        asend[q] = packed
        for i in range(1, 8):
            a_msg(q, i).start()
        arecv[q, pl.ds(me8, 1)] = packed[None]

    def stage1(q):
        rcopy(arecv.at[q, 0:7], arecv.at[q, 0:7], a_s.at[0], a_r.at[q], dp, v).wait_recv()
        got = arecv[q]
        bits = jnp.sum(got, axis=0)
        (m0, t0, o0), (m1, t1, o1) = combine(got)
        packed = jnp.concatenate([m0, t0, o0, bits[3:4], m1, t1, o1, bits[7:8]], axis=0)
        bsend[q] = packed
        for i in range(1, N_Z):
            b_msg(q, i).start()
        brecv[q, pl.ds(z, 1)] = packed[None]

    def stage2(q):
        rcopy(brecv.at[q, 0:7], brecv.at[q, 0:7], b_s.at[0], b_r.at[q], dp, v).wait_recv()
        rows8 = []
        for half, (mx, tot, mom) in enumerate(combine(brecv[q])):
            weight = bsend[q, 4 * half + 3:4 * half + 4, :] * scale
            gap = mom / tot
            rows8 += [mx, weight / tot, gap, weight * (gap - mx - jnp.log(tot))]
        cols = jnp.concatenate(rows8 + [jnp.zeros((120, 128), F32)], axis=0).T
        ycol[...] = cols
        lane_f = lax.broadcasted_iota(jnp.int32, (128, 128), 1)
        for half in range(2):
            lossbuf[q, half * 128:(half + 1) * 128, :] = jnp.where(
                lane_f == FB, cols[:, 4 * half + 3:4 * half + 4], 0.0)

            def rows(r, _, half=half):
                yat = pl.ds(pl.multiple_of(r * ROWS, ROWS), ROWS)
                at = pl.ds(pl.multiple_of(half * 128 + r * ROWS, ROWS), ROWS)
                rr = half * 4 + r
                yc = ycol[yat, :]
                mx, inv, gap = (yc[:, 4 * half + k:4 * half + k + 1] for k in range(3))
                logits = lbuf[q, at, :]
                targets = tbuf[q, rr // 2, pl.ds(rr % 2 * 2, 2)].reshape(ROWS, CB).astype(F32)
                gbuf[at, :] = (jnp.exp(logits - mx) * inv * (logits - targets - gap)).astype(BF16)
                return 0

            lax.fori_loop(0, 4, rows, 0, unroll=4)

        out = lax.dot_general(
            wbuf[...].reshape(FEAT, CB), gbuf[...], (((1,), (1,)), ((), ())), preferred_element_type=F32)
        part[q] = out.reshape(N_Z, 2, FB, TOK)
        c_msg(q).start()

    low_lane = lax.broadcasted_iota(jnp.int32, (FB, 128), 1) < 64

    def stage3(q):
        c_msg(q).wait_recv()

        def pair(p, _):
            for h in range(2):
                even = part[q, 2 * p, c, :, h * 128:(h + 1) * 128] + corebuf[q, 2 * p, :, h * 128:(h + 1) * 128]
                odd_z = part[q, 2 * p + 1, c, :, h * 128:(h + 1) * 128] + corebuf[q, 2 * p + 1, :, h * 128:(h + 1) * 128]
                xs[q, 2 * h, p] = jnp.where(low_lane, even, pltpu.roll(odd_z, 64, 1)).astype(BF16)
                xs[q, 2 * h + 1, p] = jnp.where(low_lane, pltpu.roll(even, 64, 1), odd_z).astype(BF16)
            return 0

        lax.fori_loop(0, 4, pair, 0)
        for i in (1, 3, 2):
            x_msg(q, i).start()

    def stage4(q):
        total = xs[q, x].astype(F32)
        rcopy(xr.at[q, 0:3], xr.at[q, 0:3], x_s.at[0], x_r.at[q], dp, v).wait_recv()
        for i in (1, 3, 2):
            total += xr[q, (x + i) % 4].astype(F32)
        zs[q] = total.astype(BF16)
        for i in (1, 7, 2, 6, 3, 5, 4):
            z_msg(q, i).start()

    def stage5(q):
        total = zs[q, z // 2].astype(F32)
        rcopy(zr.at[q, 0:7], zr.at[q, 0:7], z_s.at[0], z_r.at[q], dp, v).wait_recv()
        for i in range(1, N_Z):
            total += zr[q, (z + i) % N_Z].astype(F32)
        tr[...] = jnp.concatenate([total, jnp.zeros((128 - FB, 128), F32)], axis=0).T
        mine_rows = tr[pl.ds(pl.multiple_of(z % 2 * 64, 64), 64), :] + lossbuf[q, pl.ds(pl.multiple_of(x * 64, 64), 64), :]
        fs[q] = mine_rows

        @pl.when(y == q)
        def _():
            fr[pl.ds(y, 1)] = mine_rows[None]

        @pl.when(y != q)
        def _():
            f_msg(q).start()

    stages = [stage0, stage1, stage2, stage3, stage4, stage5]

    def tick(tau, _):
        for s in (0, 1, 3, 4, 5, 2):
            q = tau - s

            @pl.when((q >= 0) & (q < Q))
            def _(s=s, q=q):
                stages[s](q)
        return 0

    lax.fori_loop(0, Q + len(stages) - 1, tick, 0)
    rcopy(fr.at[0:3], fr.at[0:3], f_s.at[0], f_r.at[0], dp, v).wait_recv()
    out_ref[...] = fr[...].reshape(TOK, 128)

    @pl.when(x == v % 4)
    def _():
        rcopy(hsend.at[0:15 * SHARE], hsend.at[0:15 * SHARE], hd_s.at[0], hd_r.at[0], dp, v).wait_send()

    for whole, ss, rs in (
        (wbuf.at[0:15], w_s, w_r), (posbuf.at[0:15], pos_s, pos_r), (hbuf.at[:, 0:15], h_s, hc_r),
        (tbuf.at[:, :, 0:3], t_s, t_r), (arecv.at[:, 0:7], a_s, a_r), (brecv.at[:, 0:7], b_s, b_r),
        (corebuf, c_s, c_r), (xr.at[:, 0:3], x_s, x_r), (zr.at[:, 0:7], z_s, z_r), (fr.at[0:3], f_s, f_r),
    ):
        rcopy(whole, whole, ss.at[0], rs.at[0], dp, v).wait_send()


def finish(rows_ref, place_ref, grad_ref, loss_ref):
    rows = rows_ref[...]
    hi = rows.astype(BF16)
    rest = rows - hi.astype(F32)
    mid = rest.astype(BF16)
    low = (rest - mid.astype(F32)).astype(BF16)
    placed = jnp.zeros((TOK, 128), F32)
    for piece in (low, mid, hi):
        placed += jnp.dot(place_ref[...], piece, preferred_element_type=F32)
    turned = placed.T
    grad_ref[...] = turned[0:FB, :]
    loss_ref[...] = turned[FB:FB + 1, :]


def per_device(hidden_states, head_weight, teacher_logprobs, teacher_dest, lengths):
    vm = pltpu.VMEM
    dma = pltpu.SemaphoreType.DMA
    rows, place = pl.pallas_call(
        kernel,
        out_shape=(jax.ShapeDtypeStruct((TOK, 128), F32), jax.ShapeDtypeStruct((TOK, TOK), BF16)),
        in_specs=[pl.BlockSpec(memory_space=pltpu.VMEM), pl.BlockSpec(memory_space=pltpu.SMEM)]
        + [pl.BlockSpec(memory_space=pl.ANY)] * 3,
        out_specs=(pl.BlockSpec(memory_space=pltpu.VMEM), pl.BlockSpec(memory_space=pltpu.VMEM)),
        scratch_shapes=[
            vm((TOK, VSH), BF16),
            vm((TOK, FEAT), BF16),
            vm((N_DP, FB, CB), BF16),
            vm((Q, 4, SHARE, VSH), BF16),
            vm((Q, 4, 4, SHARE, CB), BF16),
            vm((TOK, FEAT), BF16),
            vm((Q, N_DP, SHARE, FEAT), BF16),
            vm((N_DP, 8, 128), F32),
            vm((N_DP, 8, 128), F32),
            vm((TOK, TOK), BF16),
            vm((Q, 8, 128), F32),
            vm((Q, TOK, CB), F32),
            vm((TOK, CB), BF16),
            vm((TOK, 128), F32),
            vm((128, 128), F32),
            vm((Q, TOK, 128), F32),
            vm((Q, 8, 128), F32),
            vm((Q, 8, 8, 128), F32),
            vm((Q, 8, 128), F32),
            vm((Q, N_Z, 8, 128), F32),
            vm((Q, N_Z, 2, FB, TOK), F32),
            vm((Q, N_Z, FB, TOK), F32),
            vm((Q, 4, 4, FB, 128), BF16),
            vm((Q, 4, 4, FB, 128), BF16),
            vm((Q, 4, FB, 128), BF16),
            vm((Q, N_Z, FB, 128), BF16),
            vm((128, 128), F32),
            vm((Q, 64, 128), F32),
            vm((4, 64, 128), F32),
            dma((3,)),
            dma((1,)), dma((NC,)), dma((NC, 2)), dma((NC,)),
            dma((1,)), dma((1,)),
            dma((1,)), dma((Q,)),
            dma((1,)), dma((2, 2, 4)), dma((1,)),
            dma((1,)), dma((Q,)),
            dma((1,)), dma((Q,)),
            dma((1,)), dma((Q,)),
            dma((1,)), dma((Q,)),
            dma((1,)), dma((Q,)),
            dma((1,)), dma((Q,)),
            dma((1,)), dma((Q,)),
        ],
        compiler_params=pltpu.CompilerParams(
            collective_id=0, has_side_effects=True, vmem_limit_bytes=58 * 2**20),
        name="distill",
    )(teacher_dest.reshape(2, 128), lengths, hidden_states, head_weight, teacher_logprobs)
    grad, loss = pl.pallas_call(
        finish,
        out_shape=(jax.ShapeDtypeStruct((FB, TOK), F32), jax.ShapeDtypeStruct((1, TOK), F32)),
        name="finish",
    )(rows, place)
    return grad.T, loss.reshape(TOK)


def solution(mesh):
    placed = (P("dp", None), P("dp", "vocab"), P("dp", "vocab"), P("dp"), P("dp"))
    return jax.shard_map(
        per_device,
        mesh=mesh,
        in_specs=placed,
        out_specs=(P("dp", "vocab"), P("dp")),
        check_vma=False,
    )
```

```python
import functools

import jax
import jax.numpy as jnp
from jax import lax
from jax.experimental import pallas as pl
from jax.experimental.pallas import tpu as pltpu
from jax.sharding import PartitionSpec as P

MESH = pl.DeviceIdType.MESH
SLOT = 128
N_DP = 16
N_V = 16
N_Z = 8
TOK = 256
SHARE = 16
FEAT = 1280
FB = 80
VSH = 4864
CB = 1280
CC, NC = 256, 5
Q = 4
ROWS = 32
BIG = 1e30
OFFSET = (0, 1, 3, 4, 6, 8)
ZQ = 0
F32, BF16 = jnp.float32, jnp.bfloat16


def col_start(x):
    return pl.multiple_of((19 * (x // 2) + 9 * (x % 2)) * 128, 128)


def kernel(dest_ref, len_ref, h_hbm, w_hbm, t_hbm, out_ref, place_ref,
           tin, hin, wbuf, tord, tbuf, hsend, hbuf, possend, posbuf, sel, vbuf,
           lbuf, gbuf, statcol, ycol, lossbuf, asend, arecv, bsend, brecv,
           part, corebuf, xs, xr, zs, zr, tr, fs, fr,
           lsem, w_s, wx_r, wf_r, w_r, pos_s, pos_r, hd_s, hd_r, h_s, hz_r, hc_r,
           t_s, t_r, a_s, a_r, b_s, b_r, c_s, c_r, x_s, x_r, z_s, z_r, f_s, f_r):
    dp = lax.axis_index("dp")
    v = lax.axis_index("vocab")
    x, y = dp % 4, dp // 4
    z, c = v // 2, v % 2

    def rcopy(src, dst, ss, rs, d, vv):
        return pltpu.make_async_remote_copy(
            src_ref=src, dst_ref=dst, send_sem=ss, recv_sem=rs, device_id=(d, vv), device_id_type=MESH)

    bar = pltpu.get_barrier_semaphore()

    def greet(d, vv):
        pl.semaphore_signal(bar, inc=1, device_id=(d, vv), device_id_type=MESH)

    for i in range(1, N_DP):
        greet((dp + i) % N_DP, v)
    for i in range(4):
        greet(y * 4 + (x + i) % 4, z * 2 + 1 - c)
    for i in range(1, N_Z):
        greet(dp, (z + i) % N_Z * 2 + c)

    own_w = pltpu.make_async_copy(w_hbm.at[:, pl.ds(col_start(x), CB)], wbuf.at[dp], lsem.at[0])
    get_t = pltpu.make_async_copy(t_hbm, tin, lsem.at[1])
    get_h = pltpu.make_async_copy(h_hbm, hin, lsem.at[2])
    get_t.start()
    own_w.start()
    get_h.start()

    drow = jnp.concatenate([dest_ref[0:1, :], dest_ref[1:2, :]], axis=1)
    grp = lax.shift_right_logical(drow, 8)
    pos = (drow & 255).astype(F32)
    member = (grp == lax.broadcasted_iota(jnp.int32, (N_DP, TOK), 0)).astype(BF16)
    upper = (lax.broadcasted_iota(jnp.int32, (TOK, TOK), 0)
             <= lax.broadcasted_iota(jnp.int32, (TOK, TOK), 1)).astype(BF16)
    rank = jnp.dot(member, upper, preferred_element_type=F32)
    slot = lax.broadcasted_iota(jnp.int32, (TOK, N_DP), 0)
    spread = (slot // SHARE == lax.broadcasted_iota(jnp.int32, (TOK, N_DP), 1)).astype(BF16)
    member_s = jnp.dot(spread, member, preferred_element_type=F32)
    rank_s = jnp.dot(spread, rank.astype(BF16), preferred_element_type=F32)
    want = (lax.broadcasted_iota(jnp.int32, (TOK, TOK), 0) % SHARE + 1).astype(F32)
    chosen = jnp.where((member_s > 0.5) & (rank_s == want), 1.0, 0.0)
    sel[...] = chosen.astype(BF16)
    sent = jnp.sum(chosen * pos, axis=1, keepdims=True)
    lane0 = dp % 8 * SHARE
    lane_s = lax.broadcasted_iota(jnp.int32, (TOK, 128), 1)
    slot_s = lax.broadcasted_iota(jnp.int32, (TOK, 128), 0)
    laid = jnp.where(lane_s == lane0 + slot_s % SHARE, sent, 0.0).astype(BF16)
    by_group = (lax.broadcasted_iota(jnp.int32, (N_DP, TOK), 1) // SHARE
                == lax.broadcasted_iota(jnp.int32, (N_DP, TOK), 0)).astype(BF16)
    rows_out = jnp.dot(by_group, laid, preferred_element_type=F32)
    sub = lax.broadcasted_iota(jnp.int32, (N_DP, 8, 128), 1)
    lane3 = lax.broadcasted_iota(jnp.int32, (N_DP, 8, 128), 2)
    mine = (lane3 >= lane0) & (lane3 < lane0 + SHARE)
    len0 = jnp.minimum(len_ref[0], SLOT).astype(F32)
    len1 = jnp.minimum(len_ref[1], SLOT).astype(F32)
    possend[...] = jnp.where(sub == 0, rows_out.reshape(N_DP, 1, 128), jnp.where(
        mine, jnp.where(sub == 1, len0, jnp.where(sub == 2, len1, 0.0)), 0.0))

    def pos_msg(i):
        d = (dp + i) % N_DP
        return rcopy(possend.at[d], posbuf.at[dp], pos_s.at[0], pos_r.at[0], d, v)

    def cut(j):
        return pl.ds(j * CC, CC)

    def w_cols(xt, j):
        return pl.ds(pl.multiple_of(col_start(xt) + j * CC, 128), CC)

    def w_x(j, i):
        xt = (x + i) % 4
        return rcopy(w_hbm.at[:, w_cols(xt, j)], wbuf.at[dp, :, cut(j)], w_s.at[0], wx_r.at[j], y * 4 + xt, v)

    def y_to(i):
        return (y + i) % 4 * 4 + x

    def w_sem(j, k, i):
        if i == 1 and k in (0, 1):
            return wf_r.at[j, 0]
        if i == 3 and k in (2, 3):
            return wf_r.at[j, 1]
        return w_r.at[j]

    def w_own_y(j, i):
        return rcopy(w_hbm.at[:, w_cols(x, j)], wbuf.at[dp, :, cut(j)], w_s.at[0], w_sem(j, 0, i), y_to(i), v)

    def w_row_y(j, k, i):
        b = y * 4 + (x + k) % 4
        return rcopy(wbuf.at[b, :, cut(j)], wbuf.at[b, :, cut(j)], w_s.at[0], w_sem(j, k, i), y_to(i), v)

    def w_fwd(j, k, i):
        b = (y + 4 - i) % 4 * 4 + (x + k) % 4
        return rcopy(wbuf.at[b, :, cut(j)], wbuf.at[b, :, cut(j)], w_s.at[0], w_r.at[j], y_to(i), v)

    def w_arrived(j, n, sem):
        rcopy(wbuf.at[0:n, :, cut(j)], wbuf.at[0:n, :, cut(j)], w_s.at[0], sem, dp, v).wait_recv()

    pl.semaphore_wait(bar, 15 + 4 + 7)
    for i in range(1, N_DP):
        pos_msg(i).start()
    for j in range(NC):
        for i in (1, 3, 2):
            w_x(j, i).start()
        for i in (1, 3):
            w_own_y(j, i).start()
    posbuf[pl.ds(dp, 1)] = possend[pl.ds(dp, 1)]

    def unit(vv):
        return vv % 4 * 4 + vv // 4

    own_w.wait()

    def w_pass_x(j):
        w_arrived(j, 3, wx_r.at[j])
        for k in (1, 3, 2):
            for i in (1, 3):
                w_row_y(j, k, i).start()

    def w_pass_y(j):
        for way, (ks, i) in enumerate((((0, 1), 1), ((3, 2), 3))):
            w_arrived(j, 2, wf_r.at[j, way])
            for k in ks:
                w_fwd(j, k, i).start()

    w_pass_x(0)
    rcopy(possend.at[0:15], posbuf.at[0:15], pos_s.at[0], pos_r.at[0], dp, v).wait_recv()
    low_t = jnp.sum(posbuf[0:8], axis=0)
    high_t = jnp.sum(posbuf[8:16], axis=0)
    seen = jnp.concatenate([low_t, high_t], axis=1)
    place = (lax.broadcasted_iota(jnp.int32, (TOK, TOK), 0).astype(F32) == seen[0:1, :]).astype(BF16)
    place_ref[...] = place
    get_h.wait()
    for j in range(5):
        hsend[:, j * 256:(j + 1) * 256] = lax.dot_general(
            place, hin[:, j * 256:(j + 1) * 256], (((0,), (0,)), ((), ())), preferred_element_type=F32).astype(BF16)

    def h_msg(i):
        d = (dp + i) % N_DP
        at = pl.ds(pl.multiple_of((d // 4 * 4 + v // 4) * SHARE, SHARE), SHARE)
        return rcopy(hsend.at[at], hbuf.at[y, unit(v)], hd_s.at[0], hd_r.at[y], d, v)

    @pl.when(x == v % 4)
    def _():
        for i in range(1, N_DP):
            h_msg(i).start()
        hbuf[pl.ds(y, 1), pl.ds(unit(v), 1)] = hsend[
            pl.ds(pl.multiple_of((y * 4 + v // 4) * SHARE, SHARE), SHARE)].reshape(1, 1, SHARE, FEAT)

    w_pass_x(1)
    get_t.wait()

    def order(j, _):
        cols = pl.ds(pl.multiple_of(j * 256, 256), 256)
        res = jnp.dot(sel[...], tin[:, cols], preferred_element_type=F32).astype(BF16)
        tord[:, :, :, cols] = res.reshape(Q, 4, SHARE, 256)
        return 0

    lax.fori_loop(0, VSH // 256, order, 0)

    def t_msg(q, i):
        xt = (x + i) % 4
        return rcopy(tord.at[q, :, :, pl.ds(col_start(xt), CB)], tbuf.at[q, :, x], t_s.at[0], t_r.at[q], y * 4 + xt, v)

    t_own = pltpu.make_async_copy(tord.at[:, :, :, pl.ds(col_start(x), CB)], tbuf.at[:, :, x], lsem.at[1])
    t_own.start()
    w_pass_x(2)

    sent_row = jnp.broadcast_to(sent, (TOK, 128)).T[0:1, :]
    sent_in = jnp.where(sent_row >= SLOT, sent_row - SLOT, sent_row)
    valid = (sent_in < jnp.where(sent_row >= SLOT, seen[2:3, :], seen[1:2, :])).astype(F32)
    eighth = (lax.broadcasted_iota(jnp.int32, (8, TOK), 1) // 32
              == lax.broadcasted_iota(jnp.int32, (8, TOK), 0)).astype(F32)
    to_lane = (lane_s == slot_s // SHARE % 2 * 64 + x * SHARE + slot_s % SHARE).astype(BF16)
    valid8 = jnp.dot((eighth * valid).astype(BF16), to_lane, preferred_element_type=F32)
    valid8 = jnp.where(c == 0, valid8, 0.0)
    sub8 = lax.broadcasted_iota(jnp.int32, (8, 128), 0)
    for q in range(Q):
        vbuf[q] = jnp.where(sub8 == 3, valid8[2 * q:2 * q + 1, :], jnp.where(
            sub8 == 7, valid8[2 * q + 1:2 * q + 2, :], 0.0))
    count = jnp.sum(seen[1:3, :], keepdims=True) * (1.0 / SHARE)
    scale = float(TOK * N_DP) / count

    def h_z(q, b, i, s):
        at = hbuf.at[q, unit(b)]
        return rcopy(at, at, h_s.at[0], hz_r.at[q, i // 4, s], dp, (z + i) % N_Z * 2 + c)

    def h_c(q, b):
        at = hbuf.at[q, unit(b)]
        return rcopy(at, at, h_s.at[0], hc_r.at[0], dp, z * 2 + 1 - c)

    def h_first(q):
        @pl.when((x != v % 4) | (y != q))
        def _():
            rcopy(hsend.at[pl.ds(0, SHARE)], hbuf.at[q, unit(v)], hd_s.at[0], hd_r.at[q], dp, v).wait_recv()
        h_z(q, v, 1, 0).start()
        h_z(q, v, N_Z - 1, 0).start()
        h_c(q, v).start()

    def h_steps(s):
        def step(q, _):
            for way, i in ((0, 1), (1, N_Z - 1)):
                def piece(way=way, i=i):
                    b = (v + N_V + (2 * s if way else -2 * s)) % N_V
                    h_z(q, b, i, s - 1).wait_recv()
                    if s < 3:
                        h_z(q, b, i, s).start()
                    elif s == 3:
                        pl.when(q % 2 == way)(lambda: h_z(q, b, i, s).start())
                    h_c(q, b).start()

                if s < 4:
                    piece()
                else:
                    pl.when(q % 2 == way)(piece)
            return 0

        lax.fori_loop(0, Q, step, 0)

    def t_send(q):
        for i in (1, 3, 2):
            t_msg(q, i).start()

    t_send(0)
    w_pass_x(3)
    w_pass_x(4)
    t_send(1)
    for q in range(Q):
        h_first(q)
    w_pass_y(0)
    h_steps(1)
    w_pass_y(1)
    w_pass_y(2)
    h_steps(2)
    t_send(2)
    w_pass_y(3)
    h_steps(3)
    w_pass_y(4)
    h_steps(4)
    t_send(3)
    rcopy(hbuf.at[:, 0:8], hbuf.at[:, 0:8], h_s.at[0], hc_r.at[0], dp, v).wait_recv()

    odd = x % 2
    def logit_chunk(j, _):
        at = pl.ds(pl.multiple_of(j * CC, CC), CC)
        rcopy(wbuf.at[0:8, :, at], wbuf.at[0:8, :, at], w_s.at[0], w_r.at[j], dp, v).wait_recv()
        hidden = (lax.broadcasted_iota(jnp.int32, (2 * TOK, CC), 1) < 128) & (odd == 1) & (j == 0)

        def half(h, _):
            out = jnp.dot(hbuf[pl.ds(h * 2, 2)].reshape(2 * TOK, FEAT), wbuf[:, :, at].reshape(FEAT, CC),
                          preferred_element_type=F32)
            lbuf[pl.ds(h * 2, 2), :, at] = jnp.where(hidden, -BIG, out).reshape(2, TOK, CC)
            return 0

        return lax.fori_loop(0, 2, half, 0)

    lax.fori_loop(0, NC, logit_chunk, 0)

    lane_r = lax.broadcasted_iota(jnp.int32, (ROWS, 128), 1)
    me8 = x * 2 + c

    t_own.wait()

    def a_msg(q, i):
        k = (me8 + i) % 8
        return rcopy(asend.at[q], arecv.at[q, me8], a_s.at[0], a_r.at[q], y * 4 + k // 2, z * 2 + k % 2)

    def b_msg(q, i):
        return rcopy(bsend.at[q], brecv.at[q, z], b_s.at[0], b_r.at[q], dp, (z + i) % N_Z * 2 + c)

    def c_msg(q):
        return rcopy(part.at[q, :, 1 - c], corebuf.at[q], c_s.at[0], c_r.at[q], dp, z * 2 + 1 - c)

    def x_msg(q, i):
        xt = (x + i) % 4
        return rcopy(xs.at[q, xt], xr.at[q, x], x_s.at[0], x_r.at[q], y * 4 + xt, v)

    def z_msg(q, i):
        zt = (z + i) % N_Z
        return rcopy(zs.at[q, zt // 2], zr.at[q, z], z_s.at[0], z_r.at[q], dp, zt * 2 + c)

    def f_msg(q):
        return rcopy(fs.at[q], fr.at[y], f_s.at[0], f_r.at[0], q * 4 + x, v)

    def combine(got):
        halves = []
        for r in (0, 4):
            mxs = got[:, r:r + 1, :]
            mx = jnp.max(mxs, axis=0)
            ratio = jnp.exp(mxs - mx[None])
            halves.append((mx, jnp.sum(ratio * got[:, r + 1:r + 2, :], axis=0),
                           jnp.sum(ratio * got[:, r + 2:r + 3, :], axis=0)))
        return halves

    def stage0(q):
        rcopy(tbuf.at[q, :, 0:3], tbuf.at[q, :, 0:3], t_s.at[0], t_r.at[q], dp, v).wait_recv()

        def rows(r, _):
            at = pl.ds(pl.multiple_of(r * ROWS, ROWS), ROWS)
            logits = lbuf[q, at, :]
            targets = tbuf[q, r // 2, pl.ds(r % 2 * 2, 2)].reshape(ROWS, CB).astype(F32)
            mx = jnp.max(logits, axis=1, keepdims=True)
            e = jnp.exp(logits - mx)
            tot = jnp.sum(e, axis=1, keepdims=True)
            mom = jnp.sum(e * (logits - targets), axis=1, keepdims=True)
            base = r // 4 * 4
            statcol[at, :] = jnp.where(lane_r == base, mx, jnp.where(
                lane_r == base + 1, tot, jnp.where(lane_r == base + 2, mom, 0.0)))
            return 0

        lax.fori_loop(0, TOK // ROWS, rows, 0, unroll=4)
        packed = (statcol[0:128, :] + statcol[128:256, :]).T[0:8, :] + vbuf[q]
        asend[q] = packed
        for i in range(1, 8):
            a_msg(q, i).start()
        arecv[q, pl.ds(me8, 1)] = packed[None]

    def stage1(q):
        rcopy(arecv.at[q, 0:7], arecv.at[q, 0:7], a_s.at[0], a_r.at[q], dp, v).wait_recv()
        got = arecv[q]
        bits = jnp.sum(got, axis=0)
        (m0, t0, o0), (m1, t1, o1) = combine(got)
        packed = jnp.concatenate([m0, t0, o0, bits[3:4], m1, t1, o1, bits[7:8]], axis=0)
        bsend[q] = packed
        for i in range(1, N_Z):
            b_msg(q, i).start()
        brecv[q, pl.ds(z, 1)] = packed[None]

    def stage2(q):
        rcopy(brecv.at[q, 0:7], brecv.at[q, 0:7], b_s.at[0], b_r.at[q], dp, v).wait_recv()
        rows8 = []
        for half, (mx, tot, mom) in enumerate(combine(brecv[q])):
            weight = bsend[q, 4 * half + 3:4 * half + 4, :] * scale
            gap = mom / tot
            rows8 += [mx, weight / tot, gap, weight * (gap - mx - jnp.log(tot))]
        cols = jnp.concatenate(rows8 + [jnp.zeros((120, 128), F32)], axis=0).T
        ycol[...] = cols
        lane_f = lax.broadcasted_iota(jnp.int32, (128, 128), 1)
        for half in range(2):
            lossbuf[q, half * 128:(half + 1) * 128, :] = jnp.where(
                lane_f == FB, cols[:, 4 * half + 3:4 * half + 4], 0.0)

            def rows(r, _, half=half):
                yat = pl.ds(pl.multiple_of(r * ROWS, ROWS), ROWS)
                at = pl.ds(pl.multiple_of(half * 128 + r * ROWS, ROWS), ROWS)
                rr = half * 4 + r
                yc = ycol[yat, :]
                mx, inv, gap = (yc[:, 4 * half + k:4 * half + k + 1] for k in range(3))
                logits = lbuf[q, at, :]
                targets = tbuf[q, rr // 2, pl.ds(rr % 2 * 2, 2)].reshape(ROWS, CB).astype(F32)
                gbuf[at, :] = (jnp.exp(logits - mx) * inv * (logits - targets - gap)).astype(BF16)
                return 0

            lax.fori_loop(0, 4, rows, 0, unroll=4)

        out = lax.dot_general(
            wbuf[...].reshape(FEAT, CB), gbuf[...], (((1,), (1,)), ((), ())), preferred_element_type=F32)
        part[q] = out.reshape(N_Z, 2, FB, TOK)
        c_msg(q).start()

    low_lane = lax.broadcasted_iota(jnp.int32, (FB, 128), 1) < 64

    def deliver(q, total, half):
        tr[...] = jnp.concatenate([total, jnp.zeros((128 - FB, 128), F32)], axis=0).T
        mine_rows = tr[pl.ds(pl.multiple_of(half * 64, 64), 64), :] + lossbuf[q, pl.ds(pl.multiple_of(x * 64, 64), 64), :]
        fs[q] = mine_rows

        @pl.when(y == q)
        def _():
            fr[pl.ds(y, 1)] = mine_rows[None]

        @pl.when(y != q)
        def _():
            f_msg(q).start()

    def stage3(q):
        c_msg(q).wait_recv()

        def pair(p, _):
            for h in range(2):
                even = part[q, 2 * p, c, :, h * 128:(h + 1) * 128] + corebuf[q, 2 * p, :, h * 128:(h + 1) * 128]
                odd_z = part[q, 2 * p + 1, c, :, h * 128:(h + 1) * 128] + corebuf[q, 2 * p + 1, :, h * 128:(h + 1) * 128]
                xs[q, 2 * h, p] = jnp.where(low_lane, even, pltpu.roll(odd_z, 64, 1)).astype(BF16)
                xs[q, 2 * h + 1, p] = jnp.where(low_lane, pltpu.roll(even, 64, 1), odd_z).astype(BF16)
            return 0

        lax.fori_loop(0, 4, pair, 0)
        for i in (1, 3, 2):
            x_msg(q, i).start()

    def stage4(q):
        total = xs[q, x].astype(F32)
        rcopy(xr.at[q, 0:3], xr.at[q, 0:3], x_s.at[0], x_r.at[q], dp, v).wait_recv()
        for i in (1, 3, 2):
            total += xr[q, (x + i) % 4].astype(F32)
        zs[q] = total.astype(BF16)
        for i in (1, 7, 2, 6, 3, 5, 4):
            z_msg(q, i).start()

    def stage5(q):
        total = zs[q, z // 2].astype(F32)
        rcopy(zr.at[q, 0:7], zr.at[q, 0:7], z_s.at[0], z_r.at[q], dp, v).wait_recv()
        for i in range(1, N_Z):
            total += zr[q, (z + i) % N_Z].astype(F32)
        deliver(q, total, z % 2)

    stages = (stage0, stage1, stage2, stage3, stage4, stage5)
    stages_z = {}

    def tick(tau, _):
        for s in (0, 1, 2, 3, 4, 5):
            q = tau - OFFSET[s]
            if s in stages_z and ZQ:
                @pl.when((q >= 0) & (q < ZQ))
                def _(s=s, q=q):
                    stages_z[s](q)

            @pl.when((q >= (ZQ if s in stages_z else 0)) & (q < Q))
            def _(s=s, q=q):
                stages[s](q)
        return 0

    lax.fori_loop(0, Q + OFFSET[-1], tick, 0)
    rcopy(fr.at[0:3], fr.at[0:3], f_s.at[0], f_r.at[0], dp, v).wait_recv()
    out_ref[...] = fr[...].reshape(TOK, 128)

    @pl.when(x == v % 4)
    def _():
        rcopy(hsend.at[0:15 * SHARE], hsend.at[0:15 * SHARE], hd_s.at[0], hd_r.at[0], dp, v).wait_send()

    for whole, ss, rs in (
        (wbuf.at[0:15], w_s, w_r), (posbuf.at[0:15], pos_s, pos_r), (hbuf.at[:, 0:15], h_s, hc_r),
        (tbuf.at[:, :, 0:3], t_s, t_r), (arecv.at[:, 0:7], a_s, a_r), (brecv.at[:, 0:7], b_s, b_r),
        (corebuf, c_s, c_r), (xr.at[ZQ:, 0:3], x_s, x_r), (zr.at[ZQ:, 0:7], z_s, z_r), (fr.at[0:3], f_s, f_r),
    ):
        rcopy(whole, whole, ss.at[0], rs.at[0], dp, v).wait_send()


def finish(rows_ref, place_ref, grad_ref, loss_ref):
    rows = rows_ref[...]
    hi = rows.astype(BF16)
    rest = rows - hi.astype(F32)
    mid = rest.astype(BF16)
    low = (rest - mid.astype(F32)).astype(BF16)
    placed = jnp.zeros((TOK, 128), F32)
    for piece in (low, mid, hi):
        placed += jnp.dot(place_ref[...], piece, preferred_element_type=F32)
    turned = placed.T
    grad_ref[...] = turned[0:FB, :]
    loss_ref[...] = turned[FB:FB + 1, :]


def per_device(hidden_states, head_weight, teacher_logprobs, teacher_dest, lengths):
    vm = pltpu.VMEM
    dma = pltpu.SemaphoreType.DMA
    rows, place = pl.pallas_call(
        kernel,
        out_shape=(jax.ShapeDtypeStruct((TOK, 128), F32), jax.ShapeDtypeStruct((TOK, TOK), BF16)),
        in_specs=[pl.BlockSpec(memory_space=pltpu.VMEM), pl.BlockSpec(memory_space=pltpu.SMEM)]
        + [pl.BlockSpec(memory_space=pl.ANY)] * 3,
        out_specs=(pl.BlockSpec(memory_space=pltpu.VMEM), pl.BlockSpec(memory_space=pltpu.VMEM)),
        scratch_shapes=[
            vm((TOK, VSH), BF16),
            vm((TOK, FEAT), BF16),
            vm((N_DP, FB, CB), BF16),
            vm((Q, 4, SHARE, VSH), BF16),
            vm((Q, 4, 4, SHARE, CB), BF16),
            vm((TOK, FEAT), BF16),
            vm((Q, N_DP, SHARE, FEAT), BF16),
            vm((N_DP, 8, 128), F32),
            vm((N_DP, 8, 128), F32),
            vm((TOK, TOK), BF16),
            vm((Q, 8, 128), F32),
            vm((Q, TOK, CB), F32),
            vm((TOK, CB), BF16),
            vm((TOK, 128), F32),
            vm((128, 128), F32),
            vm((Q, TOK, 128), F32),
            vm((Q, 8, 128), F32),
            vm((Q, 8, 8, 128), F32),
            vm((Q, 8, 128), F32),
            vm((Q, N_Z, 8, 128), F32),
            vm((Q, N_Z, 2, FB, TOK), F32),
            vm((Q, N_Z, FB, TOK), F32),
            vm((Q, 4, 4, FB, 128), BF16),
            vm((Q, 4, 4, FB, 128), BF16),
            vm((Q, 4, FB, 128), BF16),
            vm((Q, N_Z, FB, 128), BF16),
            vm((128, 128), F32),
            vm((Q, 64, 128), F32),
            vm((4, 64, 128), F32),
            dma((3,)),
            dma((1,)), dma((NC,)), dma((NC, 2)), dma((NC,)),
            dma((1,)), dma((1,)),
            dma((1,)), dma((Q,)),
            dma((1,)), dma((Q, 2, 4)), dma((1,)),
            dma((1,)), dma((Q,)),
            dma((1,)), dma((Q,)),
            dma((1,)), dma((Q,)),
            dma((1,)), dma((Q,)),
            dma((1,)), dma((Q,)),
            dma((1,)), dma((Q,)),
            dma((1,)), dma((Q,)),
        ],
        compiler_params=pltpu.CompilerParams(
            collective_id=0, has_side_effects=True, vmem_limit_bytes=58 * 2**20),
        name="distill",
    )(teacher_dest.reshape(2, 128), lengths, hidden_states, head_weight, teacher_logprobs)
    grad, loss = pl.pallas_call(
        finish,
        out_shape=(jax.ShapeDtypeStruct((FB, TOK), F32), jax.ShapeDtypeStruct((1, TOK), F32)),
        name="finish",
    )(rows, place)
    return grad.T, loss.reshape(TOK)


def solution(mesh):
    placed = (P("dp", None), P("dp", "vocab"), P("dp", "vocab"), P("dp"), P("dp"))
    return jax.shard_map(
        per_device,
        mesh=mesh,
        in_specs=placed,
        out_specs=(P("dp", "vocab"), P("dp")),
        check_vma=False,
    )
```
